256 devices in a mesh: ctx: 32 (over z, x), ep: 8 (over y, core).
Axes of the slice: x: 4, y: 4, z: 8, core: 2. Of those that a mesh axis runs over, the one named last changes fastest.
Arguments:
- lin_query: bfloat16 [8192, 4096], P('ctx', 'ep'), may hold values from -6 to 6
- lin_keys: bfloat16 [8192, 4096], P('ctx', 'ep'), may hold values from -0.5 to 0.5
- lin_values: bfloat16 [8192, 4096], P('ctx', 'ep'), may hold values from -6 to 6
- log_decay: float32 [8192, 32], P('ctx', 'ep'), may hold values from -1 to 0
- soft_query: bfloat16 [8192, 4096], P('ctx', 'ep'), may hold values from -80 to 80
- soft_keys: bfloat16 [8192, 1024], P('ctx', 'ep'), may hold values from -4 to 4
- soft_values: bfloat16 [8192, 1024], P('ctx', 'ep'), may hold values from -6 to 6
- key_lists: int32 [64, 8], P('ctx'), may hold values from 0 to 63, as said below
- moe_input: bfloat16 [512, 6144], P('ctx'), may hold values from -6 to 6
- expert_ids: int32 [512, 2], P('ctx'), may hold values from 0 to 7, all different within a row; in each aligned block of 16 rows (0 to 15, 16 to 31, ...) at most 8 rows name the same one
- expert_gates: bfloat16 [512, 2], P('ctx'), may hold values from 0.19921875 to 1
- gate_proj: bfloat16 [8, 6144, 9216], P('ep', None, 'ctx'), may hold values from -0.078125 to 0.078125
- up_proj: bfloat16 [8, 6144, 9216], P('ep', None, 'ctx'), may hold values from -0.078125 to 0.078125
- down_proj: bfloat16 [8, 9216, 6144], P('ep', 'ctx'), may hold values from -0.0625 to 0.0625
Outputs:
- lin_mixed: bfloat16 [8192, 4096], P('ctx', 'ep')
- soft_mixed: bfloat16 [8192, 4096], P('ctx', 'ep')
- expert_mixed: bfloat16 [512, 6144], P('ctx')
The draws below stay inside these ranges and needn't reach their ends.
Inputs may be any that keep to these rules, and one draw needn't show every extreme that they name: `key_lists`: the 8 key-block numbers of a query block are distinct and include the query block's own number. `expert_ids`: A token's 2 experts are distinct. Among the 16 tokens of one index of ctx no expert is named by more than 8 tokens, and in every draw some expert is named by exactly 8 of them.
All inputs are finite; a program needn't handle non-finite values.
Results may differ from the reference program's by a relative error of at most 0.023.
Values may be sent and summed in bfloat16 or wider, within the bound.
No kernel may reach another device: no remote copies, remote signals or barrier semaphores. Data moves between devices by JAX's collectives and lax.ppermute only.
A program may use at most 128 MiB of HBM per device.

```python
import math
import jax
import jax.numpy as jnp
import numpy as np
from jax import lax

D = 6144
FF = 9216
EXPERTS = 8
TOPK = 2
HD = 128
LIGHTNING_HEADS = 32
SHEADS = 32
KVHEADS = 8
BLK = 128
NSEL = 8
SEQ_DEV = 256
MOE_CTX = 16
SEQUENCE_LENGTH = 8192
CAP = 8
MTOK = 512
N_CTX = 32


def shared_keys(key):
    return jnp.clip(jax.random.normal(key, (SEQUENCE_LENGTH, KVHEADS * HD), jnp.float32), -4.0, 4.0)


def draw_log_decay(key, part):
    key = jax.random.fold_in(key, 3)
    segment_parts = jax.random.split(key, 7)
    slow_share = 0.5
    slow = jax.random.uniform(segment_parts[0], (LIGHTNING_HEADS,)) < slow_share
    fast_rate = jnp.exp(jax.random.uniform(segment_parts[1], (LIGHTNING_HEADS,), jnp.float32, jnp.log(1.0 / 50.0), jnp.log(1.0 / 30.0)))
    slow_rate = jnp.exp(jax.random.uniform(segment_parts[2], (LIGHTNING_HEADS,), jnp.float32, jnp.log(0.1), jnp.log(0.5))) * jnp.log(10.0) / SEQUENCE_LENGTH
    base = jnp.where(slow, slow_rate, fast_rate)
    device_count = SEQUENCE_LENGTH // SEQ_DEV
    device_factor = jnp.exp(jax.random.uniform(segment_parts[3], (device_count, LIGHTNING_HEADS), jnp.float32, jnp.log(0.6), jnp.log(1.6)))
    device_rows = jnp.repeat(device_factor, SEQ_DEV, axis=0)
    jitter = jax.random.uniform(segment_parts[4], (SEQUENCE_LENGTH, LIGHTNING_HEADS), jnp.float32, 0.5, 1.5)
    decay_rates = base[None, :] * device_rows * jitter
    segment_list = jax.random.uniform(segment_parts[5], (SEQUENCE_LENGTH, LIGHTNING_HEADS)) < 3.0 / SEQUENCE_LENGTH
    segment_length = jnp.log(jax.random.uniform(segment_parts[6], (SEQUENCE_LENGTH, LIGHTNING_HEADS), jnp.float32, 0.5, 0.8))
    value_tensor = -decay_rates + jnp.where(segment_list, segment_length, 0.0)
    return jnp.clip(value_tensor, -1.0, 0.0).astype(jnp.float32)


def draw_soft_keys(key, part):
    base = shared_keys(key)
    return base.astype(jnp.bfloat16)


def draw_soft_query(key, part):
    own = jax.random.fold_in(key, 5)
    query_rows = jnp.clip(jax.random.normal(own, (SEQUENCE_LENGTH, SHEADS * HD), jnp.float32), -4.0, 4.0)
    return query_rows.astype(jnp.bfloat16)


def draw_key_lists(key, part):
    own = jax.random.fold_in(key, 9)
    count = SEQUENCE_LENGTH // BLK
    noise = jax.random.randint(own, (count, count), 0, 1 << 20)
    scores = noise * count + jnp.arange(count, dtype=jnp.int32)[None, :]
    diagonal = jnp.arange(count, dtype=jnp.int32)[:, None] == jnp.arange(count, dtype=jnp.int32)[None, :]
    scores = jnp.where(diagonal, 1 << 30, scores)
    return lax.top_k(scores, NSEL)[1].astype(jnp.int32)


def levels(rng, dims, pieces, low, top_value):
    loudness, own = 1.0, jax.random.fold_in(rng, 6)
    for axis_at, blocks in pieces:
        draws = jnp.exp(jax.random.uniform(jax.random.fold_in(own, axis_at), (blocks,), jnp.float32, low / len(pieces), top_value / len(pieces)))
        loudness = loudness * jnp.repeat(draws, dims[axis_at] // blocks).reshape([-1 if axis == axis_at else 1 for axis in range(len(dims))])
    return loudness


def routed_block(key, own, number, rows, count, top, bound, slope):
    sequence = jax.random.permutation(key, count)
    crowded, ordinary = shares(count, rows * top, bound, slope, True), shares(count, rows * top, bound, slope, False)
    places = jnp.arange(count)

    def named(lengths, offset_by):
        used = int((lengths > 0).sum())
        fixed = max(1, used // 4)
        passed = fixed + (places - fixed + offset_by * (used - fixed)) % max(1, count - fixed)
        return jnp.zeros((count,), jnp.int32).at[sequence[jnp.where(places < fixed, places, passed)]].set(jnp.asarray(lengths, jnp.int32))

    lengths = jnp.where(number % 4 == 0, named(crowded, number // 4), named(ordinary, number - number // 4 - 1))
    mixed = jax.random.permutation(jax.random.fold_in(own, 3), count)
    giver, sink = mixed[0:count // 2 * 2:2], mixed[1:count // 2 * 2:2]
    margin = jnp.minimum(lengths[giver] - 1, bound - lengths[sink]) // 2
    margin = jnp.where((giver == sequence[0]) | (sink == sequence[0]) | (lengths[sink] == 0), 0, jnp.maximum(margin, 0))
    passed = jax.random.randint(jax.random.fold_in(own, 4), (count // 2,), 0, 1 << 20) % (margin + 1)
    lengths = lengths.at[giver].add(-passed).at[sink].add(passed)
    members = jnp.searchsorted(jnp.cumsum(lengths), jnp.arange(rows * top), side="right").astype(jnp.int32)
    grid = members.reshape(top, rows).T
    grid = grid[jax.random.permutation(jax.random.fold_in(own, 1), rows)]
    offset_by = jax.random.randint(jax.random.fold_in(own, 2), (rows, 1), 0, top)
    return jnp.take_along_axis(grid, (jnp.arange(top)[None, :] + offset_by) % top, axis=1)


def shares(number_of, total, reach, lean, full):
    loads = [(1 << 20) // math.isqrt(grade ** lean) + 1 for grade in range(1, number_of + 1)]
    largest = reach if full else min(reach, max(-(-total // number_of), total * loads[0] // sum(loads)))
    least = 1 if total - largest >= number_of - 1 else 0
    given, surplus = [largest] + [least] * (number_of - 1), total - largest - least * (number_of - 1)
    while surplus > 0:
        free = [i for i in range(1, number_of) if given[i] < largest] or [i for i in range(1, number_of) if given[i] < reach]
        mass, remaining = sum([loads[i] for i in free]), surplus
        for i in free:
            addition = min(reach - given[i], max(1, remaining * loads[i] // mass), surplus)
            given[i] = given[i] + addition
            surplus = surplus - addition
    return np.array(given)


def bell_draw(rng, shape, scale, limit, cuts=(), kind=jnp.bfloat16):
    drawn = jax.random.normal(rng, shape, jnp.float32) * scale
    if len(cuts) > 0:
        drawn = levels(rng, shape, cuts, -0.22, 0.18) * drawn
    return jnp.clip(drawn, min=-limit, max=limit).astype(kind)


def setup_inputs(seed: int = 0) -> dict:
    key_of = jax.random.split(jax.random.key(seed), 15)
    lin_query = bell_draw(key_of[0], (SEQUENCE_LENGTH, LIGHTNING_HEADS * HD), 1.0, 6.0, ((0, 32), (1, 8)))
    lin_keys = bell_draw(key_of[1], (SEQUENCE_LENGTH, LIGHTNING_HEADS * HD), HD ** -0.5, 0.5, ((0, 32), (1, 8)))
    lin_values = bell_draw(key_of[2], (SEQUENCE_LENGTH, LIGHTNING_HEADS * HD), 1.0, 6.0, ((0, 32), (1, 8)))
    log_decay = draw_log_decay(jax.random.fold_in(key_of[14], 71), 0)
    soft_query = draw_soft_query(jax.random.fold_in(key_of[14], 71), 0)
    soft_keys = draw_soft_keys(jax.random.fold_in(key_of[14], 71), 0)
    soft_values = bell_draw(key_of[6], (SEQUENCE_LENGTH, KVHEADS * HD), 1.0, 6.0, ((0, 32), (1, 8)))
    key_lists = draw_key_lists(jax.random.fold_in(key_of[14], 71), 0)
    moe_input = bell_draw(key_of[8], (MTOK, D), 1.0, 6.0, ((0, 32),))
    expert_ids_keys = jax.random.split(jax.random.fold_in(key_of[9], 1), MTOK // MOE_CTX)
    expert_ids_turns = jax.random.permutation(jax.random.fold_in(key_of[9], 3), MTOK // MOE_CTX)
    expert_ids = jax.vmap(lambda own, number: routed_block(jax.random.fold_in(key_of[9], 2), own, number, MOE_CTX, EXPERTS, TOPK, CAP, 2))(expert_ids_keys, expert_ids_turns).reshape((MTOK, TOPK))
    expert_gates = jnp.clip(0.19921875 + 0.80078125 * jax.random.uniform(key_of[10], (MTOK, TOPK), jnp.float32) ** levels(key_of[10], (MTOK, TOPK), ((0, 32),), -0.2, 0.2), 0.19921875, 1.0).astype(jnp.bfloat16)
    gate_proj = bell_draw(key_of[11], (EXPERTS, D, FF), D ** -0.5, 0.078125, ((0, 8), (2, 32)))
    up_proj = bell_draw(key_of[12], (EXPERTS, D, FF), D ** -0.5, 0.078125, ((0, 8), (2, 32)))
    down_proj = bell_draw(key_of[13], (EXPERTS, FF, D), FF ** -0.5, 0.0625, ((0, 8), (1, 32)))
    return {"lin_query": lin_query, "lin_keys": lin_keys, "lin_values": lin_values, "log_decay": log_decay, "soft_query": soft_query, "soft_keys": soft_keys, "soft_values": soft_values, "key_lists": key_lists, "moe_input": moe_input, "expert_ids": expert_ids, "expert_gates": expert_gates, "gate_proj": gate_proj, "up_proj": up_proj, "down_proj": down_proj}


def to_half(value_tensor):
    rounded = value_tensor.astype(jnp.bfloat16)
    rounded = lax.optimization_barrier(rounded)
    return rounded.astype(jnp.float32)

def lightning(lin_query, lin_keys, lin_values, log_decay):
    heads = LIGHTNING_HEADS
    blocks = SEQUENCE_LENGTH // BLK
    query_rows = lin_query.reshape(blocks, BLK, heads, HD)
    key_rows = lin_keys.reshape(blocks, BLK, heads, HD)
    value_rows = lin_values.reshape(blocks, BLK, heads, HD)
    decay_rows = log_decay.reshape(blocks, BLK, heads)
    positions = jnp.arange(BLK, dtype=jnp.int32)
    causal = (positions[:, None] >= positions[None, :])[:, :, None]

    def advance(state, item):
        query_block, key_block, value_block, decay_block = item
        query_f = query_block.astype(jnp.float32)
        key_f = key_block.astype(jnp.float32)
        value_f = value_block.astype(jnp.float32)
        cumul = jnp.cumsum(decay_block, axis=0)
        spread = cumul[:, None, :] - cumul[None, :, :]
        weight = jnp.where(causal, jnp.exp(jnp.where(causal, spread, 0.0)), 0.0)
        scores = jnp.einsum('thd,shd->tsh', query_f, key_f, precision=lax.Precision.HIGHEST) * weight
        inside = jnp.einsum('tsh,she->the', to_half(scores), value_f, precision=lax.Precision.HIGHEST)
        carried_in = jnp.exp(cumul)[:, :, None] * jnp.einsum('thd,hde->the', query_f, state, precision=lax.Precision.HIGHEST)
        ending = cumul[-1]
        carried = jnp.exp(ending[None, :] - cumul)[:, :, None] * key_f
        state = jnp.exp(ending)[:, None, None] * state + jnp.einsum('shd,she->hde', to_half(carried), value_f, precision=lax.Precision.HIGHEST)
        return (state, inside + carried_in)
    start_state = jnp.zeros((heads, HD, HD), jnp.float32)
    _, output_rows = lax.scan(advance, start_state, (query_rows, key_rows, value_rows, decay_rows))
    output_rows = output_rows.reshape(SEQUENCE_LENGTH, heads, HD)
    output_rows = output_rows * lax.rsqrt(lax.optimization_barrier(jnp.mean(output_rows * output_rows, axis=-1, keepdims=True)) + 1e-05)
    return output_rows.reshape(SEQUENCE_LENGTH, heads * HD).astype(jnp.bfloat16)

def sparse_softmax(soft_query, soft_keys, soft_values, key_lists):
    groups = SHEADS // KVHEADS
    blocks = SEQUENCE_LENGTH // BLK
    scaling = float(HD) ** (-0.5)
    query_blocks = soft_query.reshape(blocks, BLK, KVHEADS, groups, HD)
    key_blocks = soft_keys.reshape(blocks, BLK, KVHEADS, HD)
    value_blocks = soft_values.reshape(blocks, BLK, KVHEADS, HD)

    def attend(item):
        query_block, picks = item
        chosen_keys = key_blocks[picks].reshape(NSEL * BLK, KVHEADS, HD).astype(jnp.float32)
        chosen_values = value_blocks[picks].reshape(NSEL * BLK, KVHEADS, HD).astype(jnp.float32)
        scores = jnp.einsum('tkgd,skd->kgts', query_block.astype(jnp.float32), chosen_keys, precision=lax.Precision.HIGHEST) * scaling
        highest = lax.optimization_barrier(jnp.max(scores, axis=-1, keepdims=True))
        weights = jnp.exp(scores - highest)
        denom = lax.optimization_barrier(jnp.sum(weights, axis=-1))
        mixed = jnp.einsum('kgts,skd->tkgd', to_half(weights), chosen_values, precision=lax.Precision.HIGHEST)
        mixed = mixed / jnp.transpose(denom, (2, 0, 1))[..., None]
        return mixed.reshape(BLK, SHEADS * HD).astype(jnp.bfloat16)
    return lax.map(attend, (query_blocks, key_lists)).reshape(SEQUENCE_LENGTH, SHEADS * HD)

def expert_layer(moe_input, expert_ids, expert_gates, gate_proj, up_proj, down_proj):
    slots = CAP * N_CTX
    share = FF // N_CTX
    gates_f = expert_gates.astype(jnp.float32)

    def one_expert(running, item):
        number, weight_gate, weight_up, weight_down = item
        match = expert_ids == number
        routed = jnp.any(match, axis=1)
        token_gate = lax.optimization_barrier(jnp.sum(jnp.where(match, gates_f, 0.0), axis=1))
        picked = jnp.nonzero(routed, size=slots, fill_value=0)[0].astype(jnp.int32)
        valid = jnp.arange(slots, dtype=jnp.int32) < jnp.sum(routed.astype(jnp.int32))
        chosen = moe_input[picked]
        gate_val = jnp.dot(chosen, weight_gate, preferred_element_type=jnp.float32)
        up_val = jnp.dot(chosen, weight_up, preferred_element_type=jnp.float32)
        hidden = (jax.nn.silu(gate_val) * up_val).astype(jnp.bfloat16)
        hidden_groups = jnp.transpose(hidden.reshape(slots, N_CTX, share), (1, 0, 2))
        down_groups = weight_down.reshape(N_CTX, share, D)

        def add_group(total, pair):
            hidden_part, down_part = pair
            partial_sum = jnp.dot(hidden_part, down_part, preferred_element_type=jnp.float32).astype(jnp.bfloat16)
            partial_sum = lax.optimization_barrier(partial_sum)
            return (total + partial_sum.astype(jnp.float32), None)
        expert_out, _ = lax.scan(add_group, jnp.zeros((slots, D), jnp.float32), (hidden_groups, down_groups))
        scaled = jnp.where(valid[:, None], token_gate[picked][:, None] * expert_out, 0.0)
        return (running.at[picked].add(scaled), None)
    numbers = jnp.arange(EXPERTS, dtype=jnp.int32)
    total, _ = lax.scan(one_expert, jnp.zeros((MTOK, D), jnp.float32), (numbers, gate_proj, up_proj, down_proj))
    return total.astype(jnp.bfloat16)

def reference(lin_query, lin_keys, lin_values, log_decay, soft_query, soft_keys, soft_values, key_lists, moe_input, expert_ids, expert_gates, gate_proj, up_proj, down_proj):
    lin_mixed = lightning(lin_query, lin_keys, lin_values, log_decay)
    soft_mixed = sparse_softmax(soft_query, soft_keys, soft_values, key_lists)
    expert_mixed = expert_layer(moe_input, expert_ids, expert_gates, gate_proj, up_proj, down_proj)
    return (lin_mixed, soft_mixed, expert_mixed)
```

```python
import functools

import jax
import jax.numpy as jnp
from jax import lax
from jax.experimental import pallas as pl
from jax.experimental.pallas import tpu as pltpu
from jax.sharding import PartitionSpec as P

HD = 128
BLK = 128
CAP = 8
F32 = jnp.float32
BF16 = jnp.bfloat16
VMEM = pl.BlockSpec(memory_space=pltpu.VMEM)
SMEM = pl.BlockSpec(memory_space=pltpu.SMEM)
PARAMS = pltpu.CompilerParams(vmem_limit_bytes=48 << 20)


def dot(a, b, dims=((1,), (0,)), precision=None):
    return lax.dot_general(a, b, (dims, ((), ())), precision=precision, preferred_element_type=F32)


def lower_ones(rows):
    at_row = lax.broadcasted_iota(jnp.int32, (rows, rows), 0)
    at_col = lax.broadcasted_iota(jnp.int32, (rows, rows), 1)
    return at_row >= at_col


def lightning_inside(query_ref, key_ref, value_ref, decay_ref, inside_ref, cumul_ref, send_ref):
    rows, heads = decay_ref.shape
    pieces = send_ref.shape[0] // heads
    depth = HD // pieces
    causal = lower_ones(rows)
    ones = causal.astype(F32)
    decay = decay_ref[...]
    cumul = dot(ones, decay, precision=lax.Precision.HIGHEST)
    cumul_rows = dot(decay, ones, ((0,), (1,)), lax.Precision.HIGHEST)
    cumul_ref[...] = cumul
    for h in range(heads):
        cols = slice(h * HD, (h + 1) * HD)
        query, key, value = query_ref[:, cols], key_ref[:, cols], value_ref[:, cols]
        along = cumul[:, h : h + 1]
        ending = cumul[rows - 1 : rows, h : h + 1]
        spread = along - cumul_rows[h : h + 1, :]
        weight = jnp.where(causal, jnp.exp(jnp.where(causal, spread, 0.0)), 0.0)
        scores = dot(query, key, ((1,), (1,))) * weight
        inside_ref[:, cols] = dot(scores.astype(BF16), value)
        carried = (jnp.exp(ending - along) * key.astype(F32)).astype(BF16)
        state = dot(carried, value, ((0,), (0,)))
        send_ref[h * pieces : (h + 1) * pieces, :depth, :] = state.astype(BF16).reshape(
            pieces, depth, HD
        )
        whole = jnp.broadcast_to(jnp.exp(ending), (depth, HD))
        first = whole.astype(BF16)
        rest = whole - first.astype(F32)
        second = rest.astype(BF16)
        third = (rest - second.astype(F32)).astype(BF16)
        place = lax.broadcasted_iota(jnp.int32, (depth, HD), 0)
        terms = jnp.where(
            place == 0,
            first.astype(F32),
            jnp.where(place == 1, second.astype(F32), jnp.where(place == 2, third.astype(F32), 0.0)),
        ).astype(BF16)
        for p in range(pieces):
            send_ref[h * pieces + p, depth:, :] = terms


def lightning_chain(got_ref, back_ref):
    places, _, _ = got_ref.shape
    depth = back_ref.shape[1]
    state = jnp.zeros((depth, HD), F32)
    for i in range(places):
        back_ref[i] = state.astype(BF16)
        block = got_ref[i].astype(F32)
        tail = block[depth:]
        whole = tail[0:1] + tail[1:2] + tail[2:3]
        state = whole * state + block[:depth]


def lightning_finish(query_ref, inside_ref, cumul_ref, state_ref, out_ref):
    heads = cumul_ref.shape[1]
    state = state_ref[...].reshape(heads * HD, HD)
    for h in range(heads):
        cols = slice(h * HD, (h + 1) * HD)
        carried = dot(query_ref[:, cols], state[h * HD : (h + 1) * HD])
        raw = inside_ref[:, cols] + jnp.exp(cumul_ref[:, h : h + 1]) * carried
        scale = lax.rsqrt(jnp.mean(raw * raw, axis=-1, keepdims=True) + 1e-05)
        out_ref[:, cols] = (raw * scale).astype(BF16)


def lightning_part(lin_query, lin_keys, lin_values, log_decay, places):
    rows, heads = log_decay.shape
    depth = heads * HD // places
    inside, cumul, send = pl.pallas_call(
        lightning_inside,
        out_shape=(
            jax.ShapeDtypeStruct((rows, heads * HD), F32),
            jax.ShapeDtypeStruct((rows, heads), F32),
            jax.ShapeDtypeStruct((places, 2 * depth, HD), BF16),
        ),
        in_specs=[VMEM] * 4,
        out_specs=(VMEM,) * 3,
        compiler_params=PARAMS,
        name="lightning_inside",
    )(lin_query, lin_keys, lin_values, log_decay)
    got = lax.all_to_all(send, "ctx", 0, 0)
    back = pl.pallas_call(
        lightning_chain,
        out_shape=jax.ShapeDtypeStruct((places, depth, HD), BF16),
        in_specs=[VMEM],
        out_specs=VMEM,
        compiler_params=PARAMS,
        name="lightning_chain",
    )(got)
    state = lax.all_to_all(back, "ctx", 0, 0)
    return pl.pallas_call(
        lightning_finish,
        out_shape=jax.ShapeDtypeStruct((rows, heads * HD), BF16),
        in_specs=[VMEM] * 4,
        out_specs=VMEM,
        compiler_params=PARAMS,
        name="lightning_finish",
    )(lin_query, inside, cumul, state)


def sparse_attention(lists_ref, query_ref, pairs_ref, out_ref, keys_ref, values_ref):
    blocks, picks = lists_ref.shape
    groups = query_ref.shape[1] // HD
    scaling = float(HD) ** (-0.5)
    for b in range(blocks):
        for n in range(picks):
            start = pl.multiple_of(lists_ref[b, n] * BLK, BLK)
            keys_ref[n * BLK : (n + 1) * BLK, :] = pairs_ref[pl.ds(start, BLK), :HD]
            values_ref[n * BLK : (n + 1) * BLK, :] = pairs_ref[pl.ds(start, BLK), HD:]
        for g in range(groups):
            cols = slice(g * HD, (g + 1) * HD)
            query = query_ref[b * BLK : (b + 1) * BLK, cols]
            scores = dot(query, keys_ref[...], ((1,), (1,))) * scaling
            weights = jnp.exp(scores - jnp.max(scores, axis=-1, keepdims=True))
            denom = jnp.sum(weights, axis=-1, keepdims=True)
            mixed = dot(weights.astype(BF16), values_ref[...])
            out_ref[b * BLK : (b + 1) * BLK, cols] = (mixed / denom).astype(BF16)


def softmax_part(soft_query, pairs, key_lists):
    picks = key_lists.shape[1]
    return pl.pallas_call(
        sparse_attention,
        out_shape=jax.ShapeDtypeStruct(soft_query.shape, BF16),
        in_specs=[SMEM, VMEM, VMEM],
        out_specs=VMEM,
        scratch_shapes=[pltpu.VMEM((picks * BLK, HD), BF16)] * 2,
        compiler_params=PARAMS,
        name="sparse_attention",
    )(key_lists, soft_query, pairs)


def pick_tokens(expert_ref, ids_ref, token_ref, out_ref):
    rows = ids_ref.shape[0]
    ids = ids_ref[...]
    match = jnp.any(ids == expert_ref[0], axis=1, keepdims=True)
    counted = jnp.broadcast_to(match.astype(F32), (rows, CAP))
    place = dot(lower_ones(rows).astype(F32), counted)
    slot = lax.broadcasted_iota(jnp.int32, (rows, CAP), 1).astype(F32) + 1.0
    onehot = jnp.where(match & (place == slot), 1.0, 0.0).astype(BF16)
    out_ref[...] = dot(onehot, token_ref[...], ((0,), (0,))).astype(BF16)


def feed_forward(slots_ref, gate_ref, up_ref, down_ref, out_ref):
    slots = slots_ref[...]
    gate_val = dot(slots, gate_ref[0])
    up_val = dot(slots, up_ref[0])
    hidden = (gate_val / (1.0 + jnp.exp(-gate_val)) * up_val).astype(BF16)
    width = 512
    for n in range(out_ref.shape[1] // width):
        cols = slice(n * width, (n + 1) * width)
        out_ref[:, cols] = dot(hidden, down_ref[0, :, cols]).astype(BF16)


def combine(ids_ref, gates_ref, sums_ref, out_ref):
    rows = ids_ref.shape[0]
    slots = sums_ref.shape[0]
    ids, gates = ids_ref[...], gates_ref[...].astype(F32)
    lane = lax.broadcasted_iota(jnp.int32, (rows, slots), 1)
    expert = lane // CAP
    slot = (lane - expert * CAP).astype(F32) + 1.0
    routed = jnp.zeros((rows, slots), F32)
    weight = jnp.zeros((rows, slots), F32)
    for k in range(ids.shape[1]):
        match = ids[:, k : k + 1] == expert
        routed = routed + jnp.where(match, 1.0, 0.0)
        weight = weight + jnp.where(match, gates[:, k : k + 1], 0.0)
    place = dot(lower_ones(rows).astype(F32), routed)
    coeff = jnp.where((routed > 0.0) & (place == slot), weight, 0.0).astype(BF16)
    out_ref[...] = dot(coeff, sums_ref[...]).astype(BF16)


def pick_part(moe_input, expert_ids):
    expert = lax.axis_index("ep").astype(jnp.int32).reshape(1)
    return pl.pallas_call(
        pick_tokens,
        out_shape=jax.ShapeDtypeStruct((CAP, moe_input.shape[1]), BF16),
        in_specs=[SMEM, VMEM, VMEM],
        out_specs=VMEM,
        compiler_params=PARAMS,
        name="pick_tokens",
    )(expert, expert_ids, moe_input)


def expert_part(all_slots, expert_ids, expert_gates, gate_proj, up_proj, down_proj, places):
    slots, width = all_slots.shape
    terms = pl.pallas_call(
        feed_forward,
        out_shape=jax.ShapeDtypeStruct((slots, width), BF16),
        in_specs=[VMEM] * 4,
        out_specs=VMEM,
        compiler_params=PARAMS,
        name="feed_forward",
    )(all_slots, gate_proj, up_proj, down_proj)
    parts = lax.all_to_all(terms.reshape(places, CAP, width), "ctx", 0, 0)
    sums = jnp.sum(parts.astype(F32), axis=0).astype(BF16)
    all_sums = lax.all_gather(sums, "ep", axis=0, tiled=True)
    return pl.pallas_call(
        combine,
        out_shape=jax.ShapeDtypeStruct((expert_ids.shape[0], width), BF16),
        in_specs=[VMEM] * 3,
        out_specs=VMEM,
        compiler_params=PARAMS,
        name="combine",
    )(expert_ids, expert_gates, all_sums)


def per_device(
    places,
    lin_query,
    lin_keys,
    lin_values,
    log_decay,
    soft_query,
    soft_keys,
    soft_values,
    key_lists,
    moe_input,
    expert_ids,
    expert_gates,
    gate_proj,
    up_proj,
    down_proj,
):
    picked = pick_part(moe_input, expert_ids)
    picked, soft_keys, soft_values = lax.optimization_barrier((picked, soft_keys, soft_values))
    all_slots = lax.all_gather(picked, "ctx", axis=0, tiled=True)
    pairs = lax.all_gather(
        jnp.concatenate([soft_keys, soft_values], axis=1), "ctx", axis=0, tiled=True
    )
    lin_mixed = lightning_part(lin_query, lin_keys, lin_values, log_decay, places)
    expert_mixed = expert_part(
        all_slots, expert_ids, expert_gates, gate_proj, up_proj, down_proj, places
    )
    soft_mixed = softmax_part(soft_query, pairs, key_lists)
    return (lin_mixed, soft_mixed, expert_mixed)


def solution(mesh):
    placed = (
        P("ctx", "ep"),
        P("ctx", "ep"),
        P("ctx", "ep"),
        P("ctx", "ep"),
        P("ctx", "ep"),
        P("ctx", "ep"),
        P("ctx", "ep"),
        P("ctx", None),
        P("ctx", None),
        P("ctx", None),
        P("ctx", None),
        P("ep", None, "ctx"),
        P("ep", None, "ctx"),
        P("ep", "ctx", None),
    )
    return jax.shard_map(
        functools.partial(per_device, mesh.shape["ctx"]),
        mesh=mesh,
        in_specs=placed,
        out_specs=(P("ctx", "ep"), P("ctx", "ep"), P("ctx", None)),
        check_vma=False,
    )
```

```python
import functools

import jax
import jax.numpy as jnp
from jax import lax
from jax.experimental import pallas as pl
from jax.experimental.pallas import tpu as pltpu
from jax.sharding import Mesh
from jax.sharding import PartitionSpec as P

HD = 128
BLK = 128
CAP = 8
F32 = jnp.float32
BF16 = jnp.bfloat16
VMEM = pl.BlockSpec(memory_space=pltpu.VMEM)
SMEM = pl.BlockSpec(memory_space=pltpu.SMEM)
ANY = pl.BlockSpec(memory_space=pl.ANY)
PARAMS = pltpu.CompilerParams(vmem_limit_bytes=16 << 20)
X = 4
CTX = ("z", "x")
CHUNKS = 6


def dot(a, b, dims=((1,), (0,)), precision=None):
    return lax.dot_general(a, b, (dims, ((), ())), precision=precision, preferred_element_type=F32)


def called(kernel, out_shape, operands, specs, after=(), scratch=(), limit=16, cost=None, name=None):
    given = len(operands)

    def body(*refs):
        kernel(*refs[:given], *refs[given + len(after) :])

    many = isinstance(out_shape, tuple)
    return pl.pallas_call(
        body,
        out_shape=out_shape,
        in_specs=list(specs) + [ANY] * len(after),
        out_specs=(VMEM,) * len(out_shape) if many else VMEM,
        scratch_shapes=scratch,
        compiler_params=pltpu.CompilerParams(vmem_limit_bytes=limit << 20),
        cost_estimate=cost,
        name=name,
    )(*operands, *after)


def lower_ones(rows):
    at_row = lax.broadcasted_iota(jnp.int32, (rows, rows), 0)
    at_col = lax.broadcasted_iota(jnp.int32, (rows, rows), 1)
    return at_row >= at_col


def lightning_inside(query_ref, key_ref, value_ref, decay_ref, inside_ref, cumul_ref, send_ref):
    heads, rows = decay_ref.shape
    pieces = send_ref.shape[0] // heads
    depth = HD // pieces
    causal = lower_ones(rows)
    ones = causal.astype(F32)
    decay = decay_ref[...]
    cumul = dot(ones, decay, ((1,), (1,)), lax.Precision.HIGHEST)
    cumul_rows = dot(decay, ones, ((1,), (1,)), lax.Precision.HIGHEST)
    cumul_ref[...] = cumul
    for h in range(heads):
        cols = slice(h * HD, (h + 1) * HD)
        query, key, value = query_ref[:, cols], key_ref[:, cols], value_ref[:, cols]
        along = cumul[:, h : h + 1]
        ending = cumul[rows - 1 : rows, h : h + 1]
        spread = along - cumul_rows[h : h + 1, :]
        weight = jnp.where(causal, jnp.exp(jnp.where(causal, spread, 0.0)), 0.0)
        scores = dot(query, key, ((1,), (1,))) * weight
        inside_ref[:, cols] = dot(scores.astype(BF16), value)
        carried = (jnp.exp(ending - along) * key.astype(F32)).astype(BF16)
        state = dot(carried, value, ((0,), (0,)))
        send_ref[h * pieces : (h + 1) * pieces, :depth, :] = state.astype(BF16).reshape(
            pieces, depth, HD
        )
        whole = jnp.broadcast_to(jnp.exp(ending), (depth, HD))
        first = whole.astype(BF16)
        rest = whole - first.astype(F32)
        second = rest.astype(BF16)
        third = (rest - second.astype(F32)).astype(BF16)
        place = lax.broadcasted_iota(jnp.int32, (depth, HD), 0)
        terms = jnp.where(
            place == 0,
            first.astype(F32),
            jnp.where(place == 1, second.astype(F32), jnp.where(place == 2, third.astype(F32), 0.0)),
        ).astype(BF16)
        for p in range(pieces):
            send_ref[h * pieces + p, depth:, :] = terms


def lightning_chain(got_ref, back_ref):
    places, _, _ = got_ref.shape
    depth = back_ref.shape[1]
    state = jnp.zeros((depth, HD), F32)
    for i in range(places):
        back_ref[i] = state.astype(BF16)
        block = got_ref[i].astype(F32)
        tail = block[depth:]
        whole = tail[0:1] + tail[1:2] + tail[2:3]
        state = whole * state + block[:depth]


def lightning_finish(query_ref, inside_ref, cumul_ref, state_ref, out_ref):
    heads = cumul_ref.shape[1]
    state = state_ref[...].reshape(heads * HD, HD)
    for h in range(heads):
        cols = slice(h * HD, (h + 1) * HD)
        carried = dot(query_ref[:, cols], state[h * HD : (h + 1) * HD])
        raw = inside_ref[:, cols] + jnp.exp(cumul_ref[:, h : h + 1]) * carried
        scale = lax.rsqrt(jnp.mean(raw * raw, axis=-1, keepdims=True) + 1e-05)
        out_ref[:, cols] = (raw * scale).astype(BF16)


def lightning_begin(lin_query, lin_keys, lin_values, log_decay, after):
    rows, heads = log_decay.shape
    places = lax.axis_size(CTX)
    return called(
        lightning_inside,
        (
            jax.ShapeDtypeStruct((rows, heads * HD), F32),
            jax.ShapeDtypeStruct((rows, heads), F32),
            jax.ShapeDtypeStruct((places, 2 * heads * HD // places, HD), BF16),
        ),
        (lin_query, lin_keys, lin_values, log_decay.T),
        [VMEM] * 4,
        after,
        name="lightning_inside",
    )


def lightning_states(got, after):
    places, rows, _ = got.shape
    out_shape = jax.ShapeDtypeStruct((places, rows // 2, HD), BF16)
    return called(lightning_chain, out_shape, (got,), [VMEM], after, name="lightning_chain")


def lightning_end(lin_query, inside, cumul, state, after):
    out_shape = jax.ShapeDtypeStruct(lin_query.shape, BF16)
    operands = (lin_query, inside, cumul, state)
    return called(lightning_finish, out_shape, operands, [VMEM] * 4, after, name="lightning_finish")


def sparse_attention(lists_ref, query_ref, pairs_ref, out_ref, keys_ref, values_ref):
    blocks, picks = lists_ref.shape
    groups = query_ref.shape[1] // HD
    scaling = float(HD) ** (-0.5)
    for b in range(blocks):
        for n in range(picks):
            start = pl.multiple_of(lists_ref[b, n] * BLK, BLK)
            keys_ref[n * BLK : (n + 1) * BLK, :] = pairs_ref[pl.ds(start, BLK), :HD]
            values_ref[n * BLK : (n + 1) * BLK, :] = pairs_ref[pl.ds(start, BLK), HD:]
        for g in range(groups):
            cols = slice(g * HD, (g + 1) * HD)
            query = query_ref[b * BLK : (b + 1) * BLK, cols]
            scores = dot(query, keys_ref[...], ((1,), (1,))) * scaling
            weights = jnp.exp(scores - jnp.max(scores, axis=-1, keepdims=True))
            denom = jnp.sum(weights, axis=-1, keepdims=True)
            mixed = dot(weights.astype(BF16), values_ref[...])
            out_ref[b * BLK : (b + 1) * BLK, cols] = (mixed / denom).astype(BF16)


def softmax_part(soft_query, pairs, key_lists, after):
    picks = key_lists.shape[1]
    return called(
        sparse_attention,
        jax.ShapeDtypeStruct(soft_query.shape, BF16),
        (key_lists, soft_query, pairs),
        [SMEM, VMEM, VMEM],
        after,
        [pltpu.VMEM((picks * BLK, HD), BF16)] * 2,
        name="sparse_attention",
    )


def shift(a, axis, by):
    size = lax.axis_size(axis)
    return lax.ppermute(a, axis, [(i, (i + by) % size) for i in range(size)])


def pick_tokens(expert_ref, ids_ref, token_ref, out_ref):
    top, rows = ids_ref.shape
    match = jnp.zeros((1, rows), F32)
    for k in range(top):
        match = match + jnp.where(ids_ref[k : k + 1, :] == expert_ref[0], 1.0, 0.0)
    match = jnp.broadcast_to(match, (CAP, rows))
    place = dot(match, lower_ones(rows).astype(F32), ((1,), (1,)))
    slot = lax.broadcasted_iota(jnp.int32, (CAP, rows), 0).astype(F32) + 1.0
    onehot = jnp.where((match > 0.0) & (place == slot), 1.0, 0.0).astype(BF16)
    out_ref[...] = dot(onehot, token_ref[...]).astype(BF16)


def feed_forward(pieces, *refs):
    gate_ref, up_ref, down_ref = refs[pieces : pieces + 3]
    leaving_refs = refs[pieces + 3 :]
    slots = jnp.concatenate([ref[...] for ref in refs[:pieces]], axis=0)
    gate_val = dot(slots, gate_ref[0], ((1,), (1,)))
    up_val = dot(slots, up_ref[0], ((1,), (1,)))
    hidden = (gate_val / (1.0 + jnp.exp(-gate_val)) * up_val).astype(BF16)
    span = X * CAP
    full = down_ref.shape[2]
    width = full // CHUNKS
    for n in range(CHUNKS):
        terms = dot(hidden, down_ref[0, :, n * width : (n + 1) * width])
        parts = []
        for k in range(X):
            rows = [terms[at + k * CAP : at + (k + 1) * CAP] for at in range(0, terms.shape[0], span)]
            parts.append(jnp.concatenate(rows, axis=0).astype(BF16))
        side = n // (CHUNKS // 2)
        at = n * width - side * (full // 2)
        ways = (0, 2, 3, 1) if side == 0 else (0, 1, 2, 3)
        for ref, k in zip(leaving_refs[4 * side : 4 * side + 4], ways, strict=True):
            ref[:, at : at + width] = parts[k]


def load(*refs):
    sems = refs[-1]
    copies = [pltpu.make_async_copy(refs[n], refs[n + 3], sems.at[n]) for n in range(3)]
    for copy in copies:
        copy.start()
    for copy in copies:
        copy.wait()


def loaded(weights, after):
    out_shape = tuple(jax.ShapeDtypeStruct(w.shape, BF16) for w in weights)
    sems = [pltpu.SemaphoreType.DMA((3,))]
    return called(load, out_shape, weights, [ANY] * 3, after, sems, name="load")


def relay(own_ref, came_ref, out_ref):
    out_ref[...] = (own_ref[...].astype(F32) + came_ref[...].astype(F32)).astype(BF16)


def add_parts(z_ref, *refs):
    out_ref = refs[-1]
    many = out_ref.shape[0]
    half = refs[0].shape[1]
    for side in range(2):
        here, direct, relayed = (ref[...].astype(F32) for ref in refs[3 * side : 3 * side + 3])
        total = here + direct + relayed
        cols = slice(side * half, (side + 1) * half)
        for m in range(many):
            away = (m + 1) // 2 if m % 2 == 0 else -((m + 1) // 2)
            place = lax.rem(z_ref[0] + away + many, many)
            out_ref[place, :, cols] = total[m * CAP : (m + 1) * CAP].astype(BF16)


def add_all(parts_ref, out_ref):
    total = parts_ref[0].astype(F32)
    for n in range(1, parts_ref.shape[0]):
        total = total + parts_ref[n].astype(F32)
    out_ref[...] = total.astype(BF16)


def stack(*refs):
    rows = [ref[...].astype(F32) for ref in refs[:-1]]
    refs[-1][...] = jnp.concatenate(rows, axis=0).astype(BF16)


def combine(expert_ref, ids_ref, gates_ref, mine_ref, other_ref, out_ref):
    rows = ids_ref.shape[0]
    slots = mine_ref.shape[0]
    turns = slots // CAP
    ids, gates = ids_ref[...], gates_ref[...].astype(F32)
    lane = lax.broadcasted_iota(jnp.int32, (rows, slots), 1)
    block = lane // CAP
    slot = (lane - block * CAP).astype(F32) + 1.0
    ones = lower_ones(rows).astype(F32)
    y, core = expert_ref[0] // 2, lax.rem(expert_ref[0], 2)
    total = jnp.zeros(out_ref.shape, F32)
    for swap, sums_ref in enumerate((mine_ref, other_ref)):
        expert = lax.rem(y - block + turns, turns) * 2 + (core + swap - 2 * core * swap)
        routed = jnp.zeros((rows, slots), F32)
        weight = jnp.zeros((rows, slots), F32)
        for k in range(ids.shape[1]):
            match = ids[:, k : k + 1] == expert
            routed = routed + jnp.where(match, 1.0, 0.0)
            weight = weight + jnp.where(match, gates[:, k : k + 1], 0.0)
        place = dot(ones, routed)
        coeff = jnp.where((routed > 0.0) & (place == slot), weight, 0.0).astype(BF16)
        total = total + dot(coeff, sums_ref[...])
    out_ref[...] = total.astype(BF16)


def pick_part(moe_input, expert_ids):
    expert = lax.axis_index("ep").astype(jnp.int32).reshape(1)
    return pl.pallas_call(
        pick_tokens,
        out_shape=jax.ShapeDtypeStruct((CAP, moe_input.shape[1]), BF16),
        in_specs=[SMEM, VMEM, VMEM],
        out_specs=VMEM,
        compiler_params=PARAMS,
        name="pick_tokens",
    )(expert, expert_ids.T, moe_input)


def expert_part(
    picked, expert_ids, expert_gates, gate_proj, up_proj, down_proj, begin, states, finish, attend
):
    width = picked.shape[1]
    weights = (jnp.swapaxes(gate_proj, 1, 2), jnp.swapaxes(up_proj, 1, 2), down_proj)
    hidden = down_proj.shape[1]

    inside, cumul, send = begin(())
    own = called(
        stack,
        jax.ShapeDtypeStruct((X * CAP, width), BF16),
        (picked, *(shift(picked, "x", k) for k in range(1, X))),
        [VMEM] * X,
        (send,),
        name="stack",
    )
    half = X * CAP // 2
    ahead1, back1 = shift(own, "z", 1), shift(own, "z", -1)
    got = lax.all_to_all(send, CTX, 0, 0)
    ahead2, back2 = shift(ahead1, "z", 1), shift(back1, "z", -1)
    spread = states(got, (ahead2, back2))
    ahead3, back3 = shift(ahead2, "z", 1), shift(back2, "z", -1)
    weights = loaded(weights, (ahead3, back3))
    far = [shift(ahead3[:half], "z", 1), shift(back3[half:], "z", -1)]
    blocks = [own, ahead1, back1, ahead2, back2, ahead3, back3] + far
    rows = sum(block.shape[0] for block in blocks)
    part = jax.ShapeDtypeStruct((rows // X, width // 2), BF16)
    leaving = called(
        functools.partial(feed_forward, len(blocks)),
        (part,) * 8,
        (*blocks, *weights),
        [VMEM] * (len(blocks) + 3),
        (spread,),
        (),
        24,
        pl.CostEstimate(
            flops=6 * rows * width * hidden,
            bytes_accessed=6 * width * hidden + 4 * rows * width,
            transcendentals=rows * hidden,
        ),
        "feed_forward",
    )
    state = lax.all_to_all(spread, CTX, 0, 0)
    parts = []
    for side in range(2):
        here, minus, plus, mine = leaving[4 * side : 4 * side + 4]
        minus, plus = shift(minus, "x", -1), shift(plus, "x", 1)
        came, direct = (minus, plus) if side == 0 else (plus, minus)
        relayed = called(relay, part, (mine, came), [VMEM] * 2, name="relay")
        parts += [here, direct, shift(relayed, "x", -1 if side == 0 else 1)]
    many = rows // X // CAP
    sums = called(
        add_parts,
        jax.ShapeDtypeStruct((many, CAP, width), BF16),
        (lax.axis_index("z").astype(jnp.int32).reshape(1), *parts),
        [SMEM] + [VMEM] * 6,
        (state,),
        name="add_parts",
    )
    lin_mixed = finish(inside, cumul, state, (sums,))
    soft_mixed = attend((sums,))
    sums = lax.all_to_all(sums, "z", 0, 0)
    total = called(
        add_all,
        jax.ShapeDtypeStruct((CAP, width), BF16),
        (sums,),
        [VMEM],
        (soft_mixed, lin_mixed),
        name="add_all",
    )
    experts = lax.axis_size("ep")
    blocks = [total]
    for k in range(1, experts // 2):
        pairs_of = [(i, (i + 2 * k) % experts) for i in range(experts)]
        blocks.append(lax.ppermute(total, "ep", pairs_of))
    mine = called(
        stack,
        jax.ShapeDtypeStruct((len(blocks) * CAP, width), BF16),
        tuple(blocks),
        [VMEM] * len(blocks),
        name="stack",
    )
    other = lax.ppermute(mine, "ep", [(i, i ^ 1) for i in range(experts)])
    expert = lax.axis_index("ep").astype(jnp.int32).reshape(1)
    mixed = called(
        combine,
        jax.ShapeDtypeStruct((expert_ids.shape[0], width), BF16),
        (expert, expert_ids, expert_gates, mine, other),
        [SMEM] + [VMEM] * 4,
        name="combine",
    )
    return mixed, (lin_mixed, soft_mixed)


def per_device(
    lin_query,
    lin_keys,
    lin_values,
    log_decay,
    soft_query,
    soft_keys,
    soft_values,
    key_lists,
    moe_input,
    expert_ids,
    expert_gates,
    gate_proj,
    up_proj,
    down_proj,
):
    picked = pick_part(moe_input, expert_ids)
    picked, soft_keys, soft_values = lax.optimization_barrier((picked, soft_keys, soft_values))
    pairs = lax.all_gather(
        jnp.concatenate([soft_keys, soft_values], axis=1), CTX, axis=0, tiled=True
    )
    begin = functools.partial(lightning_begin, lin_query, lin_keys, lin_values, log_decay)
    finish = functools.partial(lightning_end, lin_query)
    attend = functools.partial(softmax_part, soft_query, pairs, key_lists)
    expert_mixed, (lin_mixed, soft_mixed) = expert_part(
        picked,
        expert_ids,
        expert_gates,
        gate_proj,
        up_proj,
        down_proj,
        begin,
        lightning_states,
        finish,
        attend,
    )
    return (lin_mixed, soft_mixed, expert_mixed)


def solution(mesh):
    places, experts = mesh.devices.shape
    fine = Mesh(mesh.devices.reshape(places // X, X, experts), CTX + ("ep",))
    both, rows = P(CTX, "ep"), P(CTX, None)
    placed = (both,) * 7 + (rows,) * 4 + (P("ep", None, CTX),) * 2 + (P("ep", CTX, None),)
    return jax.shard_map(
        per_device,
        mesh=fine,
        in_specs=placed,
        out_specs=(both, both, rows),
        check_vma=False,
    )
```

```python
import functools

import jax
import jax.numpy as jnp
from jax import lax
from jax.experimental import pallas as pl
from jax.experimental.pallas import tpu as pltpu
from jax.sharding import Mesh
from jax.sharding import PartitionSpec as P

HD = 128
BLK = 128
CAP = 8
F32 = jnp.float32
BF16 = jnp.bfloat16
VMEM = pl.BlockSpec(memory_space=pltpu.VMEM)
SMEM = pl.BlockSpec(memory_space=pltpu.SMEM)
ANY = pl.BlockSpec(memory_space=pl.ANY)
PARAMS = pltpu.CompilerParams(vmem_limit_bytes=16 << 20)
X = 4
CTX = ("z", "x")
CHUNKS = 6


def dot(a, b, dims=((1,), (0,)), precision=None):
    return lax.dot_general(a, b, (dims, ((), ())), precision=precision, preferred_element_type=F32)


def called(kernel, out_shape, operands, specs, after=(), scratch=(), limit=16, cost=None, name=None):
    given = len(operands)

    def body(*refs):
        kernel(*refs[:given], *refs[given + len(after) :])

    many = isinstance(out_shape, tuple)
    return pl.pallas_call(
        body,
        out_shape=out_shape,
        in_specs=list(specs) + [ANY] * len(after),
        out_specs=(VMEM,) * len(out_shape) if many else VMEM,
        scratch_shapes=scratch,
        compiler_params=pltpu.CompilerParams(vmem_limit_bytes=limit << 20),
        cost_estimate=cost,
        name=name,
    )(*operands, *after)


def lower_ones(rows):
    at_row = lax.broadcasted_iota(jnp.int32, (rows, rows), 0)
    at_col = lax.broadcasted_iota(jnp.int32, (rows, rows), 1)
    return at_row >= at_col


def lightning_inside(query_ref, key_ref, value_ref, decay_ref, inside_ref, cumul_ref, send_ref):
    heads, rows = decay_ref.shape
    pieces = send_ref.shape[0] // heads
    depth = HD // pieces
    causal = lower_ones(rows)
    ones = causal.astype(F32)
    decay = decay_ref[...]
    cumul = dot(ones, decay, ((1,), (1,)), lax.Precision.HIGHEST)
    cumul_rows = dot(decay, ones, ((1,), (1,)), lax.Precision.HIGHEST)
    cumul_ref[...] = cumul
    for h in range(heads):
        cols = slice(h * HD, (h + 1) * HD)
        query, key, value = query_ref[:, cols], key_ref[:, cols], value_ref[:, cols]
        along = cumul[:, h : h + 1]
        ending = cumul[rows - 1 : rows, h : h + 1]
        spread = along - cumul_rows[h : h + 1, :]
        weight = jnp.where(causal, jnp.exp(jnp.where(causal, spread, 0.0)), 0.0)
        scores = dot(query, key, ((1,), (1,))) * weight
        inside_ref[:, cols] = dot(scores.astype(BF16), value)
        carried = (jnp.exp(ending - along) * key.astype(F32)).astype(BF16)
        state = dot(carried, value, ((0,), (0,)))
        send_ref[h * pieces : (h + 1) * pieces, :depth, :] = state.astype(BF16).reshape(
            pieces, depth, HD
        )
        whole = jnp.broadcast_to(jnp.exp(ending), (depth, HD))
        first = whole.astype(BF16)
        rest = whole - first.astype(F32)
        second = rest.astype(BF16)
        third = (rest - second.astype(F32)).astype(BF16)
        place = lax.broadcasted_iota(jnp.int32, (depth, HD), 0)
        terms = jnp.where(
            place == 0,
            first.astype(F32),
            jnp.where(place == 1, second.astype(F32), jnp.where(place == 2, third.astype(F32), 0.0)),
        ).astype(BF16)
        for p in range(pieces):
            send_ref[h * pieces + p, depth:, :] = terms


def lightning_chain(got_ref, back_ref):
    places, _, _ = got_ref.shape
    depth = back_ref.shape[1]
    state = jnp.zeros((depth, HD), F32)
    for i in range(places):
        back_ref[i] = state.astype(BF16)
        block = got_ref[i].astype(F32)
        tail = block[depth:]
        whole = tail[0:1] + tail[1:2] + tail[2:3]
        state = whole * state + block[:depth]


def lightning_finish(query_ref, inside_ref, cumul_ref, state_ref, out_ref):
    heads = cumul_ref.shape[1]
    state = state_ref[...].reshape(heads * HD, HD)
    for h in range(heads):
        cols = slice(h * HD, (h + 1) * HD)
        carried = dot(query_ref[:, cols], state[h * HD : (h + 1) * HD])
        raw = inside_ref[:, cols] + jnp.exp(cumul_ref[:, h : h + 1]) * carried
        scale = lax.rsqrt(jnp.mean(raw * raw, axis=-1, keepdims=True) + 1e-05)
        out_ref[:, cols] = (raw * scale).astype(BF16)


def lightning_begin(lin_query, lin_keys, lin_values, log_decay, after):
    rows, heads = log_decay.shape
    places = lax.axis_size(CTX)
    return called(
        lightning_inside,
        (
            jax.ShapeDtypeStruct((rows, heads * HD), F32),
            jax.ShapeDtypeStruct((rows, heads), F32),
            jax.ShapeDtypeStruct((places, 2 * heads * HD // places, HD), BF16),
        ),
        (lin_query, lin_keys, lin_values, log_decay.T),
        [VMEM] * 4,
        after,
        name="lightning_inside",
    )


def lightning_states(got, after):
    places, rows, _ = got.shape
    out_shape = jax.ShapeDtypeStruct((places, rows // 2, HD), BF16)
    return called(lightning_chain, out_shape, (got,), [VMEM], after, name="lightning_chain")


def lightning_end(lin_query, inside, cumul, state, after):
    out_shape = jax.ShapeDtypeStruct(lin_query.shape, BF16)
    operands = (lin_query, inside, cumul, state)
    return called(lightning_finish, out_shape, operands, [VMEM] * 4, after, name="lightning_finish")


def sparse_attention(lists_ref, query_ref, pairs_ref, out_ref, keys_ref, values_ref):
    blocks, picks = lists_ref.shape
    groups = query_ref.shape[1] // HD
    scaling = float(HD) ** (-0.5)
    for b in range(blocks):
        for n in range(picks):
            start = pl.multiple_of(lists_ref[b, n] * BLK, BLK)
            keys_ref[n * BLK : (n + 1) * BLK, :] = pairs_ref[pl.ds(start, BLK), :HD]
            values_ref[n * BLK : (n + 1) * BLK, :] = pairs_ref[pl.ds(start, BLK), HD:]
        for g in range(groups):
            cols = slice(g * HD, (g + 1) * HD)
            query = query_ref[b * BLK : (b + 1) * BLK, cols]
            scores = dot(query, keys_ref[...], ((1,), (1,))) * scaling
            weights = jnp.exp(scores - jnp.max(scores, axis=-1, keepdims=True))
            denom = jnp.sum(weights, axis=-1, keepdims=True)
            mixed = dot(weights.astype(BF16), values_ref[...])
            out_ref[b * BLK : (b + 1) * BLK, cols] = (mixed / denom).astype(BF16)


def softmax_part(soft_query, pairs, key_lists, after):
    picks = key_lists.shape[1]
    return called(
        sparse_attention,
        jax.ShapeDtypeStruct(soft_query.shape, BF16),
        (key_lists, soft_query, pairs),
        [SMEM, VMEM, VMEM],
        after,
        [pltpu.VMEM((picks * BLK, HD), BF16)] * 2,
        name="sparse_attention",
    )


def shift(a, axis, by):
    size = lax.axis_size(axis)
    return lax.ppermute(a, axis, [(i, (i + by) % size) for i in range(size)])


def pick_tokens(expert_ref, ids_ref, token_ref, out_ref):
    top, rows = ids_ref.shape
    match = jnp.zeros((1, rows), F32)
    for k in range(top):
        match = match + jnp.where(ids_ref[k : k + 1, :] == expert_ref[0], 1.0, 0.0)
    match = jnp.broadcast_to(match, (CAP, rows))
    place = dot(match, lower_ones(rows).astype(F32), ((1,), (1,)))
    slot = lax.broadcasted_iota(jnp.int32, (CAP, rows), 0).astype(F32) + 1.0
    onehot = jnp.where((match > 0.0) & (place == slot), 1.0, 0.0).astype(BF16)
    out_ref[...] = dot(onehot, token_ref[...]).astype(BF16)


def feed_forward(pieces, *refs):
    gate_ref, up_ref, down_ref = refs[pieces : pieces + 3]
    leaving_refs = refs[pieces + 3 :]
    slots = jnp.concatenate([ref[...] for ref in refs[:pieces]], axis=0)
    gate_val = dot(slots, gate_ref[0], ((1,), (1,)))
    up_val = dot(slots, up_ref[0], ((1,), (1,)))
    hidden = (gate_val / (1.0 + jnp.exp(-gate_val)) * up_val).astype(BF16)
    span = X * CAP
    full = down_ref.shape[2]
    width = full // CHUNKS
    for n in range(CHUNKS):
        terms = dot(hidden, down_ref[0, :, n * width : (n + 1) * width])
        parts = []
        for k in range(X):
            rows = [terms[at + k * CAP : at + (k + 1) * CAP] for at in range(0, terms.shape[0], span)]
            parts.append(jnp.concatenate(rows, axis=0).astype(BF16))
        side = n // (CHUNKS // 2)
        at = n * width - side * (full // 2)
        ways = (0, 2, 3, 1) if side == 0 else (0, 1, 2, 3)
        for ref, k in zip(leaving_refs[4 * side : 4 * side + 4], ways, strict=True):
            ref[:, at : at + width] = parts[k]


def cut(ahead_ref, back_ref, first_ref, second_ref):
    half = first_ref.shape[0]
    first_ref[...] = ahead_ref[:half]
    second_ref[...] = back_ref[half:]


def load(*refs):
    sems = refs[-1]
    copies = [pltpu.make_async_copy(refs[n], refs[n + 3], sems.at[n]) for n in range(3)]
    for copy in copies:
        copy.start()
    for copy in copies:
        copy.wait()


def loaded(weights, after):
    out_shape = tuple(jax.ShapeDtypeStruct(w.shape, BF16) for w in weights)
    sems = [pltpu.SemaphoreType.DMA((3,))]
    return called(load, out_shape, weights, [ANY] * 3, after, sems, name="load")


def relay(own_ref, came_ref, out_ref):
    out_ref[...] = (own_ref[...].astype(F32) + came_ref[...].astype(F32)).astype(BF16)


def add_parts(z_ref, *refs):
    out_ref = refs[-1]
    many = out_ref.shape[0]
    half = refs[0].shape[1]
    for side in range(2):
        here, direct, relayed = (ref[...].astype(F32) for ref in refs[3 * side : 3 * side + 3])
        total = here + direct + relayed
        cols = slice(side * half, (side + 1) * half)
        for m in range(many):
            away = (m + 1) // 2 if m % 2 == 0 else -((m + 1) // 2)
            place = lax.rem(z_ref[0] + away + many, many)
            out_ref[place, :, cols] = total[m * CAP : (m + 1) * CAP].astype(BF16)


def add_all(parts_ref, out_ref):
    total = parts_ref[0].astype(F32)
    for n in range(1, parts_ref.shape[0]):
        total = total + parts_ref[n].astype(F32)
    out_ref[...] = total.astype(BF16)


def stack(*refs):
    rows = [ref[...].astype(F32) for ref in refs[:-1]]
    refs[-1][...] = jnp.concatenate(rows, axis=0).astype(BF16)


def combine(expert_ref, ids_ref, gates_ref, mine_ref, other_ref, out_ref):
    rows = ids_ref.shape[0]
    slots = mine_ref.shape[0]
    turns = slots // CAP
    ids, gates = ids_ref[...], gates_ref[...].astype(F32)
    lane = lax.broadcasted_iota(jnp.int32, (rows, slots), 1)
    block = lane // CAP
    slot = (lane - block * CAP).astype(F32) + 1.0
    ones = lower_ones(rows).astype(F32)
    y, core = expert_ref[0] // 2, lax.rem(expert_ref[0], 2)
    total = jnp.zeros(out_ref.shape, F32)
    for swap, sums_ref in enumerate((mine_ref, other_ref)):
        expert = lax.rem(y - block + turns, turns) * 2 + (core + swap - 2 * core * swap)
        routed = jnp.zeros((rows, slots), F32)
        weight = jnp.zeros((rows, slots), F32)
        for k in range(ids.shape[1]):
            match = ids[:, k : k + 1] == expert
            routed = routed + jnp.where(match, 1.0, 0.0)
            weight = weight + jnp.where(match, gates[:, k : k + 1], 0.0)
        place = dot(ones, routed)
        coeff = jnp.where((routed > 0.0) & (place == slot), weight, 0.0).astype(BF16)
        total = total + dot(coeff, sums_ref[...])
    out_ref[...] = total.astype(BF16)


def pick_part(moe_input, expert_ids):
    expert = lax.axis_index("ep").astype(jnp.int32).reshape(1)
    return pl.pallas_call(
        pick_tokens,
        out_shape=jax.ShapeDtypeStruct((CAP, moe_input.shape[1]), BF16),
        in_specs=[SMEM, VMEM, VMEM],
        out_specs=VMEM,
        compiler_params=PARAMS,
        name="pick_tokens",
    )(expert, expert_ids.T, moe_input)


def expert_part(
    picked, expert_ids, expert_gates, gate_proj, up_proj, down_proj, begin, states, finish, attend
):
    width = picked.shape[1]
    weights = (jnp.swapaxes(gate_proj, 1, 2), jnp.swapaxes(up_proj, 1, 2), down_proj)
    hidden = down_proj.shape[1]

    inside, cumul, send = begin(())
    own = called(
        stack,
        jax.ShapeDtypeStruct((X * CAP, width), BF16),
        (picked, *(shift(picked, "x", k) for k in range(1, X))),
        [VMEM] * X,
        (send,),
        name="stack",
    )
    half = X * CAP // 2
    ahead1, back1 = shift(own, "z", 1), shift(own, "z", -1)
    got = lax.all_to_all(send, CTX, 0, 0)
    ahead2, back2 = shift(ahead1, "z", 1), shift(back1, "z", -1)
    spread = states(got, (ahead1, back1))
    state = lax.all_to_all(spread, CTX, 0, 0)
    ahead3, back3 = shift(ahead2, "z", 1), shift(back2, "z", -1)
    weights = loaded(weights, (ahead3, back3, state))
    halves = (jax.ShapeDtypeStruct((half, width), BF16),) * 2
    first, second = called(cut, halves, (ahead3, back3), [VMEM] * 2, (), name="cut")
    far = [shift(first, "z", 1), shift(second, "z", -1)]
    blocks = [own, ahead1, back1, ahead2, back2, ahead3, back3] + far
    rows = sum(block.shape[0] for block in blocks)
    part = jax.ShapeDtypeStruct((rows // X, width // 2), BF16)
    leaving = called(
        functools.partial(feed_forward, len(blocks)),
        (part,) * 8,
        (*blocks, *weights),
        [VMEM] * (len(blocks) + 3),
        (state,),
        (),
        24,
        pl.CostEstimate(
            flops=6 * rows * width * hidden,
            bytes_accessed=6 * width * hidden + 4 * rows * width,
            transcendentals=rows * hidden,
        ),
        "feed_forward",
    )
    parts = []
    for side in range(2):
        here, minus, plus, mine = leaving[4 * side : 4 * side + 4]
        minus, plus = shift(minus, "x", -1), shift(plus, "x", 1)
        came, direct = (minus, plus) if side == 0 else (plus, minus)
        relayed = called(relay, part, (mine, came), [VMEM] * 2, name="relay")
        parts += [here, direct, shift(relayed, "x", -1 if side == 0 else 1)]
    many = rows // X // CAP
    sums = called(
        add_parts,
        jax.ShapeDtypeStruct((many, CAP, width), BF16),
        (lax.axis_index("z").astype(jnp.int32).reshape(1), *parts),
        [SMEM] + [VMEM] * 6,
        name="add_parts",
    )
    lin_mixed = finish(inside, cumul, state, (sums,))
    soft_mixed = attend((sums,))
    sums = lax.all_to_all(sums, "z", 0, 0)
    total = called(
        add_all,
        jax.ShapeDtypeStruct((CAP, width), BF16),
        (sums,),
        [VMEM],
        (soft_mixed, lin_mixed),
        name="add_all",
    )
    experts = lax.axis_size("ep")
    blocks = [total]
    for k in range(1, experts // 2):
        pairs_of = [(i, (i + 2 * k) % experts) for i in range(experts)]
        blocks.append(lax.ppermute(total, "ep", pairs_of))
    mine = called(
        stack,
        jax.ShapeDtypeStruct((len(blocks) * CAP, width), BF16),
        tuple(blocks),
        [VMEM] * len(blocks),
        name="stack",
    )
    other = lax.ppermute(mine, "ep", [(i, i ^ 1) for i in range(experts)])
    expert = lax.axis_index("ep").astype(jnp.int32).reshape(1)
    mixed = called(
        combine,
        jax.ShapeDtypeStruct((expert_ids.shape[0], width), BF16),
        (expert, expert_ids, expert_gates, mine, other),
        [SMEM] + [VMEM] * 4,
        name="combine",
    )
    return mixed, (lin_mixed, soft_mixed)


def per_device(
    lin_query,
    lin_keys,
    lin_values,
    log_decay,
    soft_query,
    soft_keys,
    soft_values,
    key_lists,
    moe_input,
    expert_ids,
    expert_gates,
    gate_proj,
    up_proj,
    down_proj,
):
    picked = pick_part(moe_input, expert_ids)
    picked, soft_keys, soft_values = lax.optimization_barrier((picked, soft_keys, soft_values))
    pairs = lax.all_gather(
        jnp.concatenate([soft_keys, soft_values], axis=1), CTX, axis=0, tiled=True
    )
    begin = functools.partial(lightning_begin, lin_query, lin_keys, lin_values, log_decay)
    finish = functools.partial(lightning_end, lin_query)
    attend = functools.partial(softmax_part, soft_query, pairs, key_lists)
    expert_mixed, (lin_mixed, soft_mixed) = expert_part(
        picked,
        expert_ids,
        expert_gates,
        gate_proj,
        up_proj,
        down_proj,
        begin,
        lightning_states,
        finish,
        attend,
    )
    return (lin_mixed, soft_mixed, expert_mixed)


def solution(mesh):
    places, experts = mesh.devices.shape
    fine = Mesh(mesh.devices.reshape(places // X, X, experts), CTX + ("ep",))
    both, rows = P(CTX, "ep"), P(CTX, None)
    placed = (both,) * 7 + (rows,) * 4 + (P("ep", None, CTX),) * 2 + (P("ep", CTX, None),)
    return jax.shard_map(
        per_device,
        mesh=fine,
        in_specs=placed,
        out_specs=(both, both, rows),
        check_vma=False,
    )
```

```python
import functools

import jax
import jax.numpy as jnp
from jax import lax
from jax.experimental import pallas as pl
from jax.experimental.pallas import tpu as pltpu
from jax.sharding import Mesh
from jax.sharding import PartitionSpec as P

HD = 128
BLK = 128
CAP = 8
F32 = jnp.float32
BF16 = jnp.bfloat16
VMEM = pl.BlockSpec(memory_space=pltpu.VMEM)
SMEM = pl.BlockSpec(memory_space=pltpu.SMEM)
ANY = pl.BlockSpec(memory_space=pl.ANY)
PARAMS = pltpu.CompilerParams(vmem_limit_bytes=16 << 20)
X = 4
CTX = ("z", "x")
CHUNKS = 6


def dot(a, b, dims=((1,), (0,)), precision=None):
    return lax.dot_general(a, b, (dims, ((), ())), precision=precision, preferred_element_type=F32)


def called(kernel, out_shape, operands, specs, after=(), scratch=(), limit=16, cost=None, name=None):
    given = len(operands)

    def body(*refs):
        kernel(*refs[:given], *refs[given + len(after) :])

    many = isinstance(out_shape, tuple)
    return pl.pallas_call(
        body,
        out_shape=out_shape,
        in_specs=list(specs) + [ANY] * len(after),
        out_specs=(VMEM,) * len(out_shape) if many else VMEM,
        scratch_shapes=scratch,
        compiler_params=pltpu.CompilerParams(vmem_limit_bytes=limit << 20),
        cost_estimate=cost,
        name=name,
    )(*operands, *after)


def lower_ones(rows):
    at_row = lax.broadcasted_iota(jnp.int32, (rows, rows), 0)
    at_col = lax.broadcasted_iota(jnp.int32, (rows, rows), 1)
    return at_row >= at_col


def lightning_inside(query_ref, key_ref, value_ref, decay_ref, inside_ref, cumul_ref, send_ref):
    heads, rows = decay_ref.shape
    pieces = send_ref.shape[0] // heads
    depth = HD // pieces
    causal = lower_ones(rows)
    ones = causal.astype(F32)
    decay = decay_ref[...]
    cumul = dot(ones, decay, ((1,), (1,)), lax.Precision.HIGHEST)
    cumul_rows = dot(decay, ones, ((1,), (1,)), lax.Precision.HIGHEST)
    cumul_ref[...] = cumul
    for h in range(heads):
        cols = slice(h * HD, (h + 1) * HD)
        query, key, value = query_ref[:, cols], key_ref[:, cols], value_ref[:, cols]
        along = cumul[:, h : h + 1]
        ending = cumul[rows - 1 : rows, h : h + 1]
        spread = along - cumul_rows[h : h + 1, :]
        weight = jnp.where(causal, jnp.exp(jnp.where(causal, spread, 0.0)), 0.0)
        scores = dot(query, key, ((1,), (1,))) * weight
        inside_ref[:, cols] = dot(scores.astype(BF16), value)
        carried = (jnp.exp(ending - along) * key.astype(F32)).astype(BF16)
        state = dot(carried, value, ((0,), (0,)))
        send_ref[h * pieces : (h + 1) * pieces, :depth, :] = state.astype(BF16).reshape(
            pieces, depth, HD
        )
        whole = jnp.broadcast_to(jnp.exp(ending), (depth, HD))
        first = whole.astype(BF16)
        rest = whole - first.astype(F32)
        second = rest.astype(BF16)
        third = (rest - second.astype(F32)).astype(BF16)
        place = lax.broadcasted_iota(jnp.int32, (depth, HD), 0)
        terms = jnp.where(
            place == 0,
            first.astype(F32),
            jnp.where(place == 1, second.astype(F32), jnp.where(place == 2, third.astype(F32), 0.0)),
        ).astype(BF16)
        for p in range(pieces):
            send_ref[h * pieces + p, depth:, :] = terms


def lightning_chain(got_ref, back_ref):
    places, _, _ = got_ref.shape
    depth = back_ref.shape[1]
    state = jnp.zeros((depth, HD), F32)
    for i in range(places):
        back_ref[i] = state.astype(BF16)
        block = got_ref[i].astype(F32)
        tail = block[depth:]
        whole = tail[0:1] + tail[1:2] + tail[2:3]
        state = whole * state + block[:depth]


def lightning_finish(query_ref, inside_ref, cumul_ref, state_ref, out_ref):
    heads = cumul_ref.shape[1]
    state = state_ref[...].reshape(heads * HD, HD)
    for h in range(heads):
        cols = slice(h * HD, (h + 1) * HD)
        carried = dot(query_ref[:, cols], state[h * HD : (h + 1) * HD])
        raw = inside_ref[:, cols] + jnp.exp(cumul_ref[:, h : h + 1]) * carried
        scale = lax.rsqrt(jnp.mean(raw * raw, axis=-1, keepdims=True) + 1e-05)
        out_ref[:, cols] = (raw * scale).astype(BF16)


def lightning_begin(lin_query, lin_keys, lin_values, log_decay, after):
    rows, heads = log_decay.shape
    places = lax.axis_size(CTX)
    return called(
        lightning_inside,
        (
            jax.ShapeDtypeStruct((rows, heads * HD), F32),
            jax.ShapeDtypeStruct((rows, heads), F32),
            jax.ShapeDtypeStruct((places, 2 * heads * HD // places, HD), BF16),
        ),
        (lin_query, lin_keys, lin_values, log_decay.T),
        [VMEM] * 4,
        after,
        name="lightning_inside",
    )


def lightning_states(got, after):
    places, rows, _ = got.shape
    out_shape = jax.ShapeDtypeStruct((places, rows // 2, HD), BF16)
    return called(lightning_chain, out_shape, (got,), [VMEM], after, name="lightning_chain")


def lightning_end(lin_query, inside, cumul, state, after):
    out_shape = jax.ShapeDtypeStruct(lin_query.shape, BF16)
    operands = (lin_query, inside, cumul, state)
    return called(lightning_finish, out_shape, operands, [VMEM] * 4, after, name="lightning_finish")


def sparse_attention(lists_ref, query_ref, pairs_ref, out_ref, keys_ref, values_ref):
    blocks, picks = lists_ref.shape
    groups = query_ref.shape[1] // HD
    scaling = float(HD) ** (-0.5)
    for b in range(blocks):
        for n in range(picks):
            start = pl.multiple_of(lists_ref[b, n] * BLK, BLK)
            keys_ref[n * BLK : (n + 1) * BLK, :] = pairs_ref[pl.ds(start, BLK), :HD]
            values_ref[n * BLK : (n + 1) * BLK, :] = pairs_ref[pl.ds(start, BLK), HD:]
        for g in range(groups):
            cols = slice(g * HD, (g + 1) * HD)
            query = query_ref[b * BLK : (b + 1) * BLK, cols]
            scores = dot(query, keys_ref[...], ((1,), (1,))) * scaling
            weights = jnp.exp(scores - jnp.max(scores, axis=-1, keepdims=True))
            denom = jnp.sum(weights, axis=-1, keepdims=True)
            mixed = dot(weights.astype(BF16), values_ref[...])
            out_ref[b * BLK : (b + 1) * BLK, cols] = (mixed / denom).astype(BF16)


def softmax_part(soft_query, pairs, key_lists, after):
    picks = key_lists.shape[1]
    return called(
        sparse_attention,
        jax.ShapeDtypeStruct(soft_query.shape, BF16),
        (key_lists, soft_query, pairs),
        [SMEM, VMEM, VMEM],
        after,
        [pltpu.VMEM((picks * BLK, HD), BF16)] * 2,
        name="sparse_attention",
    )


def shift(a, axis, by):
    size = lax.axis_size(axis)
    return lax.ppermute(a, axis, [(i, (i + by) % size) for i in range(size)])


def pick_tokens(expert_ref, ids_ref, token_ref, out_ref):
    top, rows = ids_ref.shape
    match = jnp.zeros((1, rows), F32)
    for k in range(top):
        match = match + jnp.where(ids_ref[k : k + 1, :] == expert_ref[0], 1.0, 0.0)
    match = jnp.broadcast_to(match, (CAP, rows))
    place = dot(match, lower_ones(rows).astype(F32), ((1,), (1,)))
    slot = lax.broadcasted_iota(jnp.int32, (CAP, rows), 0).astype(F32) + 1.0
    onehot = jnp.where((match > 0.0) & (place == slot), 1.0, 0.0).astype(BF16)
    out_ref[...] = dot(onehot, token_ref[...]).astype(BF16)


def feed_forward(pieces, *refs):
    gate_ref, up_ref, down_ref = refs[pieces : pieces + 3]
    leaving_refs = refs[pieces + 3 :]
    slots = jnp.concatenate([ref[...] for ref in refs[:pieces]], axis=0)
    gate_val = dot(slots, gate_ref[0], ((1,), (1,)))
    up_val = dot(slots, up_ref[0], ((1,), (1,)))
    hidden = (gate_val / (1.0 + jnp.exp(-gate_val)) * up_val).astype(BF16)
    span = X * CAP
    full = down_ref.shape[2]
    width = full // CHUNKS
    for n in range(CHUNKS):
        terms = dot(hidden, down_ref[0, :, n * width : (n + 1) * width])
        parts = []
        for k in range(X):
            rows = [terms[at + k * CAP : at + (k + 1) * CAP] for at in range(0, terms.shape[0], span)]
            parts.append(jnp.concatenate(rows, axis=0).astype(BF16))
        side = n // (CHUNKS // 2)
        at = n * width - side * (full // 2)
        ways = (0, 2, 3, 1) if side == 0 else (0, 1, 2, 3)
        for ref, k in zip(leaving_refs[4 * side : 4 * side + 4], ways, strict=True):
            ref[:, at : at + width] = parts[k]


def cut(ahead_ref, back_ref, first_ref, second_ref):
    half = first_ref.shape[0]
    first_ref[...] = ahead_ref[:half]
    second_ref[...] = back_ref[half:]


def load(*refs):
    sems = refs[-1]
    copies = [pltpu.make_async_copy(refs[n], refs[n + 3], sems.at[n]) for n in range(3)]
    for copy in copies:
        copy.start()
    for copy in copies:
        copy.wait()


def loaded(weights, after):
    out_shape = tuple(jax.ShapeDtypeStruct(w.shape, BF16) for w in weights)
    sems = [pltpu.SemaphoreType.DMA((3,))]
    return called(load, out_shape, weights, [ANY] * 3, after, sems, name="load")


def relay(own_ref, came_ref, out_ref):
    out_ref[...] = (own_ref[...].astype(F32) + came_ref[...].astype(F32)).astype(BF16)


def add_parts(z_ref, *refs):
    out_ref = refs[-1]
    many = out_ref.shape[0]
    half = refs[0].shape[1]
    for side in range(2):
        here, direct, relayed = (ref[...].astype(F32) for ref in refs[3 * side : 3 * side + 3])
        total = here + direct + relayed
        cols = slice(side * half, (side + 1) * half)
        for m in range(many):
            away = (m + 1) // 2 if m % 2 == 0 else -((m + 1) // 2)
            place = lax.rem(z_ref[0] + away + many, many)
            out_ref[place, :, cols] = total[m * CAP : (m + 1) * CAP].astype(BF16)


def add_all(parts_ref, out_ref):
    total = parts_ref[0].astype(F32)
    for n in range(1, parts_ref.shape[0]):
        total = total + parts_ref[n].astype(F32)
    out_ref[...] = total.astype(BF16)


def stack(*refs):
    rows = [ref[...].astype(F32) for ref in refs[:-1]]
    refs[-1][...] = jnp.concatenate(rows, axis=0).astype(BF16)


def combine(expert_ref, ids_ref, gates_ref, mine_ref, other_ref, out_ref):
    rows = ids_ref.shape[0]
    slots = mine_ref.shape[0]
    turns = slots // CAP
    ids, gates = ids_ref[...], gates_ref[...].astype(F32)
    lane = lax.broadcasted_iota(jnp.int32, (rows, slots), 1)
    block = lane // CAP
    slot = (lane - block * CAP).astype(F32) + 1.0
    ones = lower_ones(rows).astype(F32)
    y, core = expert_ref[0] // 2, lax.rem(expert_ref[0], 2)
    total = jnp.zeros(out_ref.shape, F32)
    for swap, sums_ref in enumerate((mine_ref, other_ref)):
        expert = lax.rem(y - block + turns, turns) * 2 + (core + swap - 2 * core * swap)
        routed = jnp.zeros((rows, slots), F32)
        weight = jnp.zeros((rows, slots), F32)
        for k in range(ids.shape[1]):
            match = ids[:, k : k + 1] == expert
            routed = routed + jnp.where(match, 1.0, 0.0)
            weight = weight + jnp.where(match, gates[:, k : k + 1], 0.0)
        place = dot(ones, routed)
        coeff = jnp.where((routed > 0.0) & (place == slot), weight, 0.0).astype(BF16)
        total = total + dot(coeff, sums_ref[...])
    out_ref[...] = total.astype(BF16)


def pick_part(moe_input, expert_ids):
    expert = lax.axis_index("ep").astype(jnp.int32).reshape(1)
    return pl.pallas_call(
        pick_tokens,
        out_shape=jax.ShapeDtypeStruct((CAP, moe_input.shape[1]), BF16),
        in_specs=[SMEM, VMEM, VMEM],
        out_specs=VMEM,
        compiler_params=PARAMS,
        name="pick_tokens",
    )(expert, expert_ids.T, moe_input)


def expert_part(
    picked, expert_ids, expert_gates, gate_proj, up_proj, down_proj, begin, states, finish, attend
):
    width = picked.shape[1]
    weights = (jnp.swapaxes(gate_proj, 1, 2), jnp.swapaxes(up_proj, 1, 2), down_proj)
    hidden = down_proj.shape[1]

    inside, cumul, send = begin(())
    own = called(
        stack,
        jax.ShapeDtypeStruct((X * CAP, width), BF16),
        (picked, *(shift(picked, "x", k) for k in range(1, X))),
        [VMEM] * X,
        (send,),
        name="stack",
    )
    half = X * CAP // 2
    ahead1, back1 = shift(own, "z", 1), shift(own, "z", -1)
    got = lax.all_to_all(send, CTX, 0, 0)
    ahead2, back2 = shift(ahead1, "z", 1), shift(back1, "z", -1)
    spread = states(got, (ahead1, back1))
    state = lax.all_to_all(spread, CTX, 0, 0)
    ahead3, back3 = shift(ahead2, "z", 1), shift(back2, "z", -1)
    weights = loaded(weights, (ahead3, back3, state))
    halves = (jax.ShapeDtypeStruct((half, width), BF16),) * 2
    first, second = called(cut, halves, (ahead3, back3), [VMEM] * 2, (), name="cut")
    far = [shift(first, "z", 1), shift(second, "z", -1)]
    blocks = [own, ahead1, back1, ahead2, back2, ahead3, back3] + far
    rows = sum(block.shape[0] for block in blocks)
    part = jax.ShapeDtypeStruct((rows // X, width // 2), BF16)
    leaving = called(
        functools.partial(feed_forward, len(blocks)),
        (part,) * 8,
        (*blocks, *weights),
        [VMEM] * (len(blocks) + 3),
        (state,),
        (),
        24,
        pl.CostEstimate(
            flops=6 * rows * width * hidden,
            bytes_accessed=6 * width * hidden + 4 * rows * width,
            transcendentals=rows * hidden,
        ),
        "feed_forward",
    )
    parts = []
    for side in range(2):
        here, minus, plus, mine = leaving[4 * side : 4 * side + 4]
        minus, plus = shift(minus, "x", -1), shift(plus, "x", 1)
        came, direct = (minus, plus) if side == 0 else (plus, minus)
        relayed = called(relay, part, (mine, came), [VMEM] * 2, name="relay")
        parts += [here, direct, shift(relayed, "x", -1 if side == 0 else 1)]
    many = rows // X // CAP
    sums = called(
        add_parts,
        jax.ShapeDtypeStruct((many, CAP, width), BF16),
        (lax.axis_index("z").astype(jnp.int32).reshape(1), *parts),
        [SMEM] + [VMEM] * 6,
        name="add_parts",
    )
    lin_mixed = finish(inside, cumul, state, (sums,))
    soft_mixed = attend((sums,))
    sums = lax.all_to_all(sums, "z", 0, 0)
    total = called(
        add_all,
        jax.ShapeDtypeStruct((CAP, width), BF16),
        (sums,),
        [VMEM],
        (soft_mixed, lin_mixed),
        name="add_all",
    )
    experts = lax.axis_size("ep")
    blocks = [total]
    for k in range(1, experts // 2):
        pairs_of = [(i, (i + 2 * k) % experts) for i in range(experts)]
        blocks.append(lax.ppermute(total, "ep", pairs_of))
    mine = called(
        stack,
        jax.ShapeDtypeStruct((len(blocks) * CAP, width), BF16),
        tuple(blocks),
        [VMEM] * len(blocks),
        name="stack",
    )
    other = lax.ppermute(mine, "ep", [(i, i ^ 1) for i in range(experts)])
    expert = lax.axis_index("ep").astype(jnp.int32).reshape(1)
    mixed = called(
        combine,
        jax.ShapeDtypeStruct((expert_ids.shape[0], width), BF16),
        (expert, expert_ids, expert_gates, mine, other),
        [SMEM] + [VMEM] * 4,
        name="combine",
    )
    return mixed, (lin_mixed, soft_mixed)


def per_device(
    lin_query,
    lin_keys,
    lin_values,
    log_decay,
    soft_query,
    soft_keys,
    soft_values,
    key_lists,
    moe_input,
    expert_ids,
    expert_gates,
    gate_proj,
    up_proj,
    down_proj,
):
    picked = pick_part(moe_input, expert_ids)
    pairs = lax.all_gather(
        jnp.concatenate([soft_keys, soft_values], axis=1), CTX, axis=0, tiled=True
    )
    begin = functools.partial(lightning_begin, lin_query, lin_keys, lin_values, log_decay)
    finish = functools.partial(lightning_end, lin_query)
    attend = functools.partial(softmax_part, soft_query, pairs, key_lists)
    expert_mixed, (lin_mixed, soft_mixed) = expert_part(
        picked,
        expert_ids,
        expert_gates,
        gate_proj,
        up_proj,
        down_proj,
        begin,
        lightning_states,
        finish,
        attend,
    )
    return (lin_mixed, soft_mixed, expert_mixed)


def solution(mesh):
    places, experts = mesh.devices.shape
    fine = Mesh(mesh.devices.reshape(places // X, X, experts), CTX + ("ep",))
    both, rows = P(CTX, "ep"), P(CTX, None)
    placed = (both,) * 7 + (rows,) * 4 + (P("ep", None, CTX),) * 2 + (P("ep", CTX, None),)
    return jax.shard_map(
        per_device,
        mesh=fine,
        in_specs=placed,
        out_specs=(both, both, rows),
        check_vma=False,
    )
```
